32 devices in a mesh: grp: 2 (over x), tp: 16 (over z, y, core).
Axes of the slice: x: 2, y: 2, z: 4, core: 2. Of those that a mesh axis runs over, the one named last changes fastest.
Arguments:
- hidden_in: bfloat16 [768, 8192], P('grp', 'tp'), parts along dimension 0, may hold values from -30 to 30
- norm_gain: bfloat16 [8192], P('tp'), may hold values from 0.5 to 8
- w_query: bfloat16 [8192, 8192], P('tp'), may hold values from -0.0625 to 0.0625
- b_query: bfloat16 [8192], P('tp'), may hold values from -3 to 3
- key_weight_matrix: bfloat16 [8192, 1024], P('tp'), may hold values from -0.0625 to 0.0625
- key_offset_bias: bfloat16 [1024], replicated, may hold values from -3 to 3
- value_weight_matrix: bfloat16 [8192, 1024], P('tp'), may hold values from -0.0625 to 0.0625
- value_offset_bias: bfloat16 [1024], replicated, may hold values from -3 to 3
- w_out: bfloat16 [8192, 8192], P('tp'), may hold values from -0.25 to 0.25
- lengths: int32 [4], P('grp'), parts along dimension 0, may hold values from 24 to 192, as said below
Outputs:
- layer_out: bfloat16 [768, 8192], P('grp', 'tp'), parts along dimension 0
- rotated_key_cache: bfloat16 [768, 1024], P('grp', 'tp'), parts along dimension 0
- value_cache: bfloat16 [768, 1024], P('grp', 'tp'), parts along dimension 0
The draws below stay inside these ranges and needn't reach their ends.
There are 2 independent parts, one for each index of `grp`. The reference program is written for one: setup_inputs(seed, part) draws one part's arguments, and reference() takes and returns one part's arrays. A program takes and returns all parts, laid end to end along the dimension named above; an argument that names none is the same for every part. Nothing has to cross between parts.
Inputs may be any that keep to these rules, and one draw needn't show every extreme that they name: `lengths`: at least one rollout fills all 192 slots; valid tokens lie at the start of a rollout's slots.
All inputs are finite; a program needn't handle non-finite values.
Results may differ from the reference program's by a relative error of at most 0.0055.
The reference program's roundings to bfloat16 on the way count: a program that leaves them out, or rounds other values in their place, can miss the bound.
Values may be sent and summed in bfloat16 or wider, within the bound.
A program may use at most 128 MiB of HBM per device.

```python
import jax
import jax.numpy as jnp
from jax import lax

MODEL_WIDTH = 8192
QUERY_HEADS = 64
KEY_VALUE_HEADS = 8
HEAD_WIDTH = 128
ROLLOUT_SLOTS = 192
GROUP_ROLLOUTS = 2
GROUP_TOKENS = 384


def draw_hidden_in(key, part):
    key = jax.random.fold_in(key, 11)
    key_base, key_rows, key_cols = jax.random.split(key, 3)
    low = jnp.log(0.3162)
    high = jnp.log(3.162)
    row_scale = jnp.exp(jax.random.uniform(key_rows, (GROUP_TOKENS, 1), jnp.float32, low, high))
    col_scale = jnp.exp(jax.random.uniform(key_cols, (1, MODEL_WIDTH), jnp.float32, low, high))
    sample = jnp.clip(jax.random.normal(key_base, (GROUP_TOKENS, MODEL_WIDTH), jnp.float32), -3.0, 3.0)
    return (sample * row_scale * col_scale).astype(jnp.bfloat16)


def draw_norm_gain(key, part):
    key = jax.random.fold_in(key, 23)
    sample = jax.random.uniform(key, (MODEL_WIDTH,), jnp.float32, 0.5, 1.5)
    return sample.astype(jnp.bfloat16)


def draw_lengths(key, part):
    key = jax.random.fold_in(key, 37)
    key_len, key_full = jax.random.split(key)
    drawn_lengths = jax.random.randint(key_len, (GROUP_ROLLOUTS,), ROLLOUT_SLOTS // 8, ROLLOUT_SLOTS + 1, jnp.int32)
    full_slot = jax.random.randint(key_full, (), 0, GROUP_ROLLOUTS, jnp.int32)
    return jnp.where(jnp.arange(GROUP_ROLLOUTS, dtype=jnp.int32) == full_slot, jnp.int32(ROLLOUT_SLOTS), drawn_lengths)


def raised(array, stream_key, source, target, blocks, factor):
    def block_of(position):
        return (jnp.arange(array.shape[position]) // (array.shape[position] // blocks)).reshape((-1,) + (1,) * (array.ndim - 1 - position))

    one_side = jax.random.permutation(stream_key, blocks)[block_of(target)]
    far = (block_of(target) + blocks // 2) % blocks
    return jnp.where((block_of(source) == one_side) | (block_of(source) == far), factor * array, array)


def level_of(rng, shape, cuts, smallest, largest):
    gain, own = 1.0, jax.random.fold_in(rng, 6)
    for axis_at, shards_of in cuts:
        heights = jnp.exp(jax.random.uniform(jax.random.fold_in(own, axis_at), (shards_of,), jnp.float32, smallest / len(cuts), largest / len(cuts)))
        gain = gain * jnp.repeat(heights, shape[axis_at] // shards_of).reshape([-1 if axis == axis_at else 1 for axis in range(len(shape))])
    return gain


def bell_draw(own_key, dims, spread, most, cuts=(), kind=jnp.bfloat16):
    array = spread * jax.random.normal(own_key, dims, jnp.float32)
    if cuts:
        array = array * level_of(own_key, dims, cuts, -0.22, 0.18)
    return jnp.clip(array, -most, most).astype(kind)


def gaussian_with(stream_key, shape, spread, most, shards, heavy, kind=jnp.bfloat16):
    result = spread * jax.random.normal(stream_key, shape, jnp.float32)
    if shards:
        result = result * level_of(stream_key, shape, shards, -0.22, 0.18)
    return jnp.clip(raised(result, jax.random.fold_in(stream_key, 3), *heavy), -most, most).astype(kind)


def setup_inputs(seed: int = 0, part: int = 0) -> dict:
    arg_keys = jax.random.split(jax.random.key(seed), 11)
    own_keys = jax.random.split(jax.random.fold_in(arg_keys[10], part), 11)
    hidden_in = draw_hidden_in(jax.random.fold_in(jax.random.fold_in(arg_keys[10], part), 71), part)
    norm_gain = draw_norm_gain(jax.random.fold_in(arg_keys[10], 71), part)
    w_query = bell_draw(arg_keys[2], (MODEL_WIDTH, QUERY_HEADS * HEAD_WIDTH), MODEL_WIDTH ** -0.5, 0.0625, ((0, 16),))
    b_query = bell_draw(arg_keys[3], (QUERY_HEADS * HEAD_WIDTH,), 0.5, 3.0, ((0, 16),))
    key_weight_matrix = bell_draw(arg_keys[4], (MODEL_WIDTH, KEY_VALUE_HEADS * HEAD_WIDTH), MODEL_WIDTH ** -0.5, 0.0625, ((0, 16),))
    key_offset_bias = bell_draw(arg_keys[5], (KEY_VALUE_HEADS * HEAD_WIDTH,), 0.5, 3.0)
    value_weight_matrix = bell_draw(arg_keys[6], (MODEL_WIDTH, KEY_VALUE_HEADS * HEAD_WIDTH), MODEL_WIDTH ** -0.5, 0.0625, ((0, 16),))
    value_offset_bias = bell_draw(arg_keys[7], (KEY_VALUE_HEADS * HEAD_WIDTH,), 0.5, 3.0)
    w_out = gaussian_with(arg_keys[8], (QUERY_HEADS * HEAD_WIDTH, MODEL_WIDTH), (HEAD_WIDTH * 8) ** -0.5, 0.25, ((0, 16),), (0, 1, 16, 2.0))
    lengths = draw_lengths(jax.random.fold_in(jax.random.fold_in(arg_keys[10], part), 71), part)
    return dict(hidden_in=hidden_in, norm_gain=norm_gain, w_query=w_query, b_query=b_query, key_weight_matrix=key_weight_matrix, key_offset_bias=key_offset_bias, value_weight_matrix=value_weight_matrix, value_offset_bias=value_offset_bias, w_out=w_out, lengths=lengths)


NORM_EPS = 1e-06
ROPE_BASE = 1000000.0

def rotary_tables(values, cosine_table, sine_table):
    half_dim = values.shape[-1] // 2
    first_half = values[..., :half_dim]
    second_half = values[..., half_dim:]
    turned = jnp.concatenate([-second_half, first_half], axis=-1)
    return values * cosine_table[:, None, :] + turned * sine_table[:, None, :]

def reference(hidden_in, norm_gain, w_query, b_query, key_weight_matrix, key_offset_bias, value_weight_matrix, value_offset_bias, w_out, lengths):
    full_x = hidden_in.astype(jnp.float32)
    mean_square = lax.optimization_barrier(jnp.mean(full_x * full_x, axis=-1, keepdims=True))
    normed = (full_x * lax.rsqrt(mean_square + NORM_EPS) * norm_gain.astype(jnp.float32)).astype(jnp.bfloat16)
    queries = jnp.dot(normed, w_query, preferred_element_type=jnp.float32) + b_query.astype(jnp.float32)
    key_projected_rows = jnp.dot(normed, key_weight_matrix, preferred_element_type=jnp.float32) + key_offset_bias.astype(jnp.float32)
    values = jnp.dot(normed, value_weight_matrix, preferred_element_type=jnp.float32) + value_offset_bias.astype(jnp.float32)
    positions = jnp.arange(ROLLOUT_SLOTS, dtype=jnp.int32)
    valid_token_mask = (positions[None, :] < lengths[:, None]).reshape(-1)
    pos_float = jnp.tile(positions, GROUP_ROLLOUTS).astype(jnp.float32)
    inverse_freq = jnp.power(ROPE_BASE, -2.0 * jnp.arange(HEAD_WIDTH // 2).astype(jnp.float32) / HEAD_WIDTH)
    angles = pos_float[:, None] * inverse_freq[None, :]
    cosine_table = jnp.concatenate([jnp.cos(angles), jnp.cos(angles)], axis=-1)
    sine_table = jnp.concatenate([jnp.sin(angles), jnp.sin(angles)], axis=-1)
    query_rotated = rotary_tables(queries.reshape(GROUP_TOKENS, QUERY_HEADS, HEAD_WIDTH), cosine_table, sine_table).astype(jnp.bfloat16)
    key_rotated = rotary_tables(key_projected_rows.reshape(GROUP_TOKENS, KEY_VALUE_HEADS, HEAD_WIDTH), cosine_table, sine_table).astype(jnp.bfloat16)
    value_rounded_rows = values.astype(jnp.bfloat16)
    zero_half_precision = jnp.zeros((), jnp.bfloat16)
    rotated_key_cache = jnp.where(valid_token_mask[:, None], key_rotated.reshape(GROUP_TOKENS, KEY_VALUE_HEADS * HEAD_WIDTH), zero_half_precision)
    value_cache = jnp.where(valid_token_mask[:, None], value_rounded_rows, zero_half_precision)
    head_repeat_count = QUERY_HEADS // KEY_VALUE_HEADS
    query_grouped_rows = query_rotated.reshape(GROUP_ROLLOUTS, ROLLOUT_SLOTS, KEY_VALUE_HEADS, head_repeat_count, HEAD_WIDTH).astype(jnp.float32)
    key_grouped_rows = key_rotated.reshape(GROUP_ROLLOUTS, ROLLOUT_SLOTS, KEY_VALUE_HEADS, HEAD_WIDTH).astype(jnp.float32)
    value_grouped_rows = value_rounded_rows.reshape(GROUP_ROLLOUTS, ROLLOUT_SLOTS, KEY_VALUE_HEADS, HEAD_WIDTH).astype(jnp.float32)
    scores = jnp.einsum('rtgqd,rsgd->rgqts', query_grouped_rows, key_grouped_rows) / jnp.sqrt(jnp.float32(HEAD_WIDTH))
    causal = positions[None, :] <= positions[:, None]
    scores = jnp.where(causal, scores, -jnp.inf)
    row_max = lax.optimization_barrier(jnp.max(scores, axis=-1, keepdims=True))
    weights = jnp.exp(scores - row_max)
    attn_probs = (weights / lax.optimization_barrier(jnp.sum(weights, axis=-1, keepdims=True))).astype(jnp.bfloat16)
    context = jnp.einsum('rgqts,rsgd->rtgqd', attn_probs.astype(jnp.float32), value_grouped_rows)
    valid_grid = valid_token_mask.reshape(GROUP_ROLLOUTS, ROLLOUT_SLOTS)
    context = jnp.where(valid_grid[:, :, None, None, None], context, 0.0).astype(jnp.bfloat16)
    context = context.reshape(GROUP_TOKENS, QUERY_HEADS * HEAD_WIDTH)
    attended = jnp.dot(context, w_out, preferred_element_type=jnp.float32)
    layer_out = (full_x + attended).astype(jnp.bfloat16)
    return (layer_out, rotated_key_cache, value_cache)
```

```python
import jax
import jax.numpy as jnp
import numpy as np
from jax import lax
from jax.experimental import pallas as pl
from jax.experimental.pallas import tpu as pltpu
from jax.sharding import PartitionSpec as P

QUERY_HEADS = 64
KEY_VALUE_HEADS = 8
HEAD_WIDTH = 128
ROLLOUT_SLOTS = 192
GROUP_ROLLOUTS = 2


NORM_EPS = 1e-06
ROPE_BASE = 1000000.0
MODEL_WIDTH = 8192


BF = jnp.bfloat16
F32 = jnp.float32
MESH = pl.DeviceIdType.MESH
TOKENS = GROUP_ROLLOUTS * ROLLOUT_SLOTS
PARTNERS = (1, 2, 3, 4, 8, 12)
I16 = jnp.int16
CODED = TOKENS + 16


def flip(bit, mask):
    return bit + mask - 2 * bit * mask


def dotf(a, b):
    return jnp.dot(a, b, preferred_element_type=F32)


def code(ref, x):
    top = jnp.maximum(jnp.max(jnp.abs(x), axis=0, keepdims=True), 1e-30)
    exponent = jnp.ceil(jnp.log2(top))
    ref[0:TOKENS, :] = jnp.round(x * (32000.0 * jnp.exp2(-exponent))).astype(jnp.int32).astype(I16)
    ref[TOKENS:CODED, :] = jnp.broadcast_to(exponent, (16, x.shape[1])).astype(jnp.int32).astype(I16)


def decode(ref, rows=slice(0, TOKENS), cols=slice(None)):
    exponent = ref[TOKENS:CODED, cols].astype(jnp.int32).astype(F32)[0:1, :]
    return ref[rows, cols].astype(jnp.int32).astype(F32) * (jnp.exp2(exponent) * (1.0 / 32000.0))


def rotate(x, cos, sin_signed):
    return x * cos + pltpu.roll(x, HEAD_WIDTH // 2, 1) * sin_signed


def fused(
    len_ref, x_ref, gain_ref, bq_ref, kb_ref, vb_ref, cos_ref, sin_ref, wq, wk, wv, wo,
    out_ref, kc_ref, vc_ref,
    xb, gb, nx, wqb, wkvb, wob,
    r1, r1r, r2, r2r,
    yas, yar, ybs, ybr, own, zas, zar, zbs, zbr,
    kvbuf, ctxb, yos, yor, owno, zos, zor,
    l_q, l_o, l_kv, c_send, c_recv,
    wq_s, wq_r, wo_s, wo_r, r_s, r_r,
    y_s, y_r, z_s, z_r,
):
    me = lax.axis_index("tp")
    c = lax.rem(me, 2)
    y = lax.rem(me // 2, 2)
    zl = lax.rem(me // 4, 2)
    zh = me // 8

    def place(mask):
        return 8 * flip(zh, mask // 8) + 4 * flip(zl, mask // 4 % 2) + 2 * flip(y, mask // 2 % 2) + flip(c, mask % 2)

    def to(src, dst, ssem, rsem, mask):
        return pltpu.make_async_remote_copy(
            src_ref=src, dst_ref=dst, send_sem=ssem, recv_sem=rsem,
            device_id={"tp": place(mask)}, device_id_type=MESH,
        )

    def z_mask(i):
        return 3 - i

    def column(i, my, mc):
        return pl.ds(pl.multiple_of(place(4 * z_mask(i) + 2 * my + mc) * 512, 512), 512)

    def load(w, buf, sem, i, h):
        return pltpu.make_async_copy(w.at[:, column(i, 1 - h, 0)], buf.at[c, 2 * i + h], sem.at[2 * i + h])

    def swap(w, buf, ss, rs, i, h):
        return to(w.at[:, column(i, 1 - h, 1)], buf.at[c, 2 * i + h], ss.at[2 * i + h], rs.at[2 * i + h], 1)

    barrier = pltpu.get_barrier_semaphore()
    for mask in PARTNERS:
        pl.semaphore_signal(barrier, inc=1, device_id={"tp": place(mask)}, device_id_type=MESH)

    @pl.when(c == 0)
    def _():
        pltpu.make_async_copy(wk, wkvb.at[c], l_kv).start()

    @pl.when(c == 1)
    def _():
        pltpu.make_async_copy(wv, wkvb.at[c], l_kv).start()

    @pl.loop(0, 4)
    def _(i):
        load(wq, wqb, l_q, i, 0).start()
        load(wq, wqb, l_q, i, 1).start()

    xf = x_ref[...].astype(F32)
    sq = xf * xf
    sq = (sq[:, 0:128] + sq[:, 128:256]) + (sq[:, 256:384] + sq[:, 384:512])
    r1[...] = jnp.broadcast_to(jnp.sum(sq.T, axis=0, keepdims=True), (8, TOKENS))
    xb[pl.ds(c, 1)] = x_ref[...][None]
    gb[pl.ds(c, 1)] = jnp.broadcast_to(gain_ref[...].astype(F32), (16, 512)).astype(BF)[None]

    pl.semaphore_wait(barrier, len(PARTNERS))

    for k in range(3):
        to(r1, r1r.at[k], r_s.at[k], r_r.at[k], k + 1).start()
    x_copy = to(x_ref, xb.at[c], c_send.at[0], c_recv.at[0], 1)
    g_copy = to(gb.at[c], gb.at[c], c_send.at[1], c_recv.at[1], 1)
    x_copy.start()
    g_copy.start()
    swap(wq, wqb, wq_s, wq_r, 0, 0).start()
    swap(wq, wqb, wq_s, wq_r, 0, 1).start()

    @pl.when(c == 0)
    def _():
        to(wv, wkvb.at[c], c_send.at[2], c_recv.at[2], 1).start()

    @pl.when(c == 1)
    def _():
        to(wk, wkvb.at[c], c_send.at[2], c_recv.at[2], 1).start()

    @pl.loop(1, 4)
    def _(i):
        swap(wq, wqb, wq_s, wq_r, i, 0).start()
        swap(wq, wqb, wq_s, wq_r, i, 1).start()

    for k in range(3):
        to(r1, r1r.at[k], r_s.at[k], r_r.at[k], k + 1).wait()
    r2[...] = (r1[...] + r1r[0]) + (r1r[1] + r1r[2])
    for k in range(3):
        to(r2, r2r.at[k], r_s.at[3 + k], r_r.at[3 + k], 4 * (k + 1)).start()
    for k in range(3):
        to(r2, r2r.at[k], r_s.at[3 + k], r_r.at[3 + k], 4 * (k + 1)).wait()
    total = (r2[...] + r2r[0]) + (r2r[1] + r2r[2])
    scale = lax.rsqrt(total[0:1, :] * (1.0 / MODEL_WIDTH) + NORM_EPS)
    scale = jnp.broadcast_to(scale, (128, TOKENS)).T
    x_copy.wait()
    g_copy.wait()
    for s in range(2):
        for b in range(4):
            cols = slice(128 * b, 128 * (b + 1))
            nx[s, :, cols] = (
                xb[s, :, cols].astype(F32) * scale * gb[s, 0:1, cols].astype(F32)
            ).astype(BF)

    @pl.loop(0, 4)
    def _(i):
        load(wo, wob, l_o, i, 0).start()
        load(wo, wob, l_o, i, 1).start()
        swap(wo, wob, wo_s, wo_r, i, 0).start()
        swap(wo, wob, wo_s, wo_r, i, 1).start()

    pltpu.make_async_copy(wk, wkvb.at[c], l_kv).wait()
    to(wk, wkvb.at[c], c_send.at[2], c_recv.at[2], 1).wait()

    def head(i, my):
        return pl.ds(pl.multiple_of(place(4 * z_mask(i) + 2 * my) // 2 * 128, 128), 128)

    def ya(i):
        return to(yas.at[i], yar.at[i], y_s.at[i], y_r.at[i], 2)

    def yb(i):
        return to(ybs.at[i], ybr.at[i], y_s.at[4 + i], y_r.at[4 + i], 2)

    def za(i):
        return to(zas.at[i], zar.at[i], z_s.at[i], z_r.at[i], 4 * z_mask(i))

    def zb(i):
        return to(zbs.at[i], zbr.at[i], z_s.at[3 + i], z_r.at[3 + i], 4 * z_mask(i))

    def yo(u):
        return to(yos.at[u], yor.at[u], y_s.at[8 + u], y_r.at[8 + u], 2)

    def zo(u):
        return to(zos.at[u], zor.at[u], z_s.at[6 + u], z_r.at[6 + u], 4 * z_mask(u // 2))

    left, right = slice(0, 256), slice(256, 512)

    def project(act, w, j, cols):
        return dotf(act[0], w[0, j, :, cols]) + dotf(act[1], w[1, j, :, cols])

    def project_kv(i, my):
        cols = head(i, my)
        return dotf(nx[0], wkvb[0, :, cols]) + dotf(nx[1], wkvb[1, :, cols])

    @pl.loop(0, 4)
    def _(i):
        load(wq, wqb, l_q, i, 0).wait()
        swap(wq, wqb, wq_s, wq_r, i, 0).wait()
        code(yas.at[i], project(nx, wqb, 2 * i, left))
        ya(i).start()
        code(ybs.at[i, :, 0:256], project(nx, wqb, 2 * i, right))
        code(ybs.at[i, :, 256:384], project_kv(i, 1))
        yb(i).start()

    def own_part(i):
        load(wq, wqb, l_q, i, 1).wait()
        swap(wq, wqb, wq_s, wq_r, i, 1).wait()
        own[:, left] = project(nx, wqb, 2 * i + 1, left)
        own[:, right] = project(nx, wqb, 2 * i + 1, right)
        own[:, 512:640] = project_kv(i, 0)

    @pl.loop(0, 3)
    def _(i):
        own_part(i)
        ya(i).wait()
        code(zas.at[i], own[:, left] + decode(yar.at[i]))
        za(i).start()
        yb(i).wait()
        code(zbs.at[i], own[:, 256:640] + decode(ybr.at[i]))
        zb(i).start()

    own_part(3)
    ya(3).wait()
    own[:, left] = own[:, left] + decode(yar.at[3])
    yb(3).wait()
    own[:, 256:640] = own[:, 256:640] + decode(ybr.at[3])
    for i in range(3):
        za(i).wait()
        zb(i).wait()
    kv = own[:, 512:640]
    for i in range(3):
        kv = kv + decode(zbr.at[i], cols=slice(256, 384))
    at = pl.ds(pl.multiple_of(me // 2 * HEAD_WIDTH, HEAD_WIDTH), HEAD_WIDTH)
    core = jnp.full((TOKENS, HEAD_WIDTH), c, jnp.int32)
    kv = kv + jnp.where(core == 0, kb_ref[0:1, at].astype(F32), vb_ref[0:1, at].astype(F32))
    cos, sin_signed = cos_ref[...], sin_ref[...]
    kvbuf[pl.ds(c, 1)] = jnp.where(core == 0, rotate(kv, cos, sin_signed), kv).astype(BF)[None]
    kv_copy = to(kvbuf.at[c], kvbuf.at[c], c_send.at[3], c_recv.at[3], 1)
    kv_copy.start()

    row = lax.broadcasted_iota(jnp.int32, (TOKENS, HEAD_WIDTH), 0)
    ok = row < jnp.where(row < ROLLOUT_SLOTS, len_ref[0], len_ref[1] + ROLLOUT_SLOTS)
    half = HEAD_WIDTH // 2

    def cache(x):
        x = jnp.where(ok, x.astype(F32), 0.0)
        return jnp.where(core[:, :half] == 0, x[:, :half], x[:, half:]).astype(BF)

    kv_copy.wait()
    kc_ref[...] = cache(kvbuf[0])
    vc_ref[...] = cache(kvbuf[1])

    shape = (ROLLOUT_SLOTS, ROLLOUT_SLOTS)
    causal = lax.broadcasted_iota(jnp.int32, shape, 1) <= lax.broadcasted_iota(jnp.int32, shape, 0)
    for r in range(GROUP_ROLLOUTS):
        rows = slice(ROLLOUT_SLOTS * r, ROLLOUT_SLOTS * (r + 1))
        k, v = kvbuf[0, rows, :], kvbuf[1, rows, :]
        for h in range(4):
            cols = slice(128 * h, 128 * (h + 1))
            zr, zcols = (zar, cols) if h < 2 else (zbr, slice(cols.start - 256, cols.stop - 256))
            q = own[rows, cols] + decode(zr.at[0], rows, zcols)
            q = q + (decode(zr.at[1], rows, zcols) + decode(zr.at[2], rows, zcols))
            q = q + bq_ref[0:1, cols].astype(F32)
            q = rotate(q, cos[rows], sin_signed[rows]).astype(BF)
            s = lax.dot_general(q, k, (((1,), (1,)), ((), ())), preferred_element_type=F32)
            s = jnp.where(causal, s / np.float32(np.sqrt(np.float32(HEAD_WIDTH))), -jnp.inf)
            w = jnp.exp(s - jnp.max(s, axis=1, keepdims=True))
            p = (w / jnp.sum(w, axis=1, keepdims=True)).astype(BF)
            o = jnp.where(ok[rows], dotf(p, v), 0.0).astype(BF)
            ctxb[pl.ds(c, 1), rows, cols] = o[None]
    ctx_copy = to(ctxb.at[c], ctxb.at[c], c_send.at[4], c_recv.at[4], 1)
    ctx_copy.start()
    ctx_copy.wait()

    @pl.loop(0, 4)
    def _(i):
        load(wo, wob, l_o, i, 0).wait()
        swap(wo, wob, wo_s, wo_r, i, 0).wait()
        code(yos.at[2 * i], project(ctxb, wob, 2 * i, left))
        yo(2 * i).start()
        code(yos.at[2 * i + 1], project(ctxb, wob, 2 * i, right))
        yo(2 * i + 1).start()

    def own_out(i):
        load(wo, wob, l_o, i, 1).wait()
        swap(wo, wob, wo_s, wo_r, i, 1).wait()
        owno[:, left] = project(ctxb, wob, 2 * i + 1, left)
        owno[:, right] = project(ctxb, wob, 2 * i + 1, right)

    @pl.loop(0, 3)
    def _(i):
        own_out(i)
        yo(2 * i).wait()
        code(zos.at[2 * i], owno[:, left] + decode(yor.at[2 * i]))
        zo(2 * i).start()
        yo(2 * i + 1).wait()
        code(zos.at[2 * i + 1], owno[:, right] + decode(yor.at[2 * i + 1]))
        zo(2 * i + 1).start()

    own_out(3)
    for p, cols in enumerate((left, right)):
        yo(6 + p).wait()
        att = owno[:, cols] + decode(yor.at[6 + p])
        for i in range(3):
            zo(2 * i + p).wait()
            att = att + decode(zor.at[2 * i + p])
        out_ref[:, cols] = (x_ref[:, cols].astype(F32) + att).astype(BF)


def local_fused(
    hidden_in, norm_gain, w_query, b_query, key_weight_matrix, key_offset_bias,
    value_weight_matrix, value_offset_bias, w_out, lengths,
):
    positions = np.tile(np.arange(ROLLOUT_SLOTS), GROUP_ROLLOUTS).astype(np.float64)
    freq = ROPE_BASE ** (-2.0 * np.arange(HEAD_WIDTH // 2) / HEAD_WIDTH)
    angles = positions[:, None] * freq[None, :]
    cos = np.concatenate([np.cos(angles), np.cos(angles)], axis=1).astype(np.float32)
    sin_signed = np.concatenate([-np.sin(angles), np.sin(angles)], axis=1).astype(np.float32)
    vmem = pl.BlockSpec(memory_space=pltpu.VMEM)
    hbm = pl.BlockSpec(memory_space=pl.ANY)
    sem = pltpu.SemaphoreType.DMA
    V = pltpu.VMEM
    T = TOKENS
    return pl.pallas_call(
        fused,
        out_shape=(
            jax.ShapeDtypeStruct((T, 512), BF),
            jax.ShapeDtypeStruct((T, HEAD_WIDTH // 2), BF),
            jax.ShapeDtypeStruct((T, HEAD_WIDTH // 2), BF),
        ),
        in_specs=[pl.BlockSpec(memory_space=pltpu.SMEM)] + [vmem] * 7 + [hbm] * 4,
        out_specs=(vmem, vmem, vmem),
        scratch_shapes=[
            V((2, T, 512), BF), V((2, 16, 512), BF), V((2, T, 512), BF),
            V((2, 8, 512, 512), BF), V((2, 512, 1024), BF), V((2, 8, 512, 512), BF),
            V((8, T), F32), V((3, 8, T), F32), V((8, T), F32), V((3, 8, T), F32),
            V((4, CODED, 256), I16), V((4, CODED, 256), I16), V((4, CODED, 384), I16), V((4, CODED, 384), I16),
            V((T, 640), F32),
            V((3, CODED, 256), I16), V((3, CODED, 256), I16), V((3, CODED, 384), I16), V((3, CODED, 384), I16),
            V((2, T, 128), BF), V((2, T, 512), BF),
            V((8, CODED, 256), I16), V((8, CODED, 256), I16), V((T, 512), F32),
            V((6, CODED, 256), I16), V((6, CODED, 256), I16),
            sem((8,)), sem((8,)), sem, sem((5,)), sem((5,)),
            sem((8,)), sem((8,)), sem((8,)), sem((8,)), sem((6,)), sem((6,)),
            sem((16,)), sem((16,)), sem((12,)), sem((12,)),
        ],
        compiler_params=pltpu.CompilerParams(
            collective_id=0, has_side_effects=True, vmem_limit_bytes=56 * 1024 * 1024
        ),
    )(
        lengths, hidden_in, norm_gain[None, :], b_query[None, :],
        key_offset_bias[None, :], value_offset_bias[None, :],
        jnp.asarray(cos), jnp.asarray(sin_signed),
        w_query, key_weight_matrix, value_weight_matrix, w_out,
    )


def rotary_tables(values, cosine_table, sine_table):
    half_dim = values.shape[-1] // 2
    first_half = values[..., :half_dim]
    second_half = values[..., half_dim:]
    turned = jnp.concatenate([-second_half, first_half], axis=-1)
    return values * cosine_table[:, None, :] + turned * sine_table[:, None, :]


def local(
    hidden_in,
    norm_gain,
    w_query,
    b_query,
    key_weight_matrix,
    key_offset_bias,
    value_weight_matrix,
    value_offset_bias,
    w_out,
    lengths,
):
    tensor_parallel_count = lax.axis_size("tp")
    device_place = lax.axis_index("tp")
    query_group_width = tensor_parallel_count // KEY_VALUE_HEADS
    heads_dev = QUERY_HEADS // tensor_parallel_count
    token_count = hidden_in.shape[0]
    gathered, gain_all = (
        lax.all_gather(hidden_in, "tp", axis=1, tiled=True),
        lax.all_gather(norm_gain, "tp", axis=0, tiled=True),
    )
    full_x = gathered.astype(jnp.float32)
    mean_square = jnp.mean(full_x * full_x, axis=-1, keepdims=True)
    normed = (full_x * lax.rsqrt(mean_square + NORM_EPS) * gain_all.astype(jnp.float32)).astype(
        jnp.bfloat16
    )
    local_row_count = key_weight_matrix.shape[0]
    kv_head = device_place // query_group_width
    tile_width = HEAD_WIDTH // query_group_width
    offset = device_place % query_group_width * tile_width
    positions = jnp.arange(ROLLOUT_SLOTS, dtype=jnp.int32)
    valid_grid = positions[None, :] < lengths[:, None]
    valid_token_mask = valid_grid.reshape(-1)
    zero_half_precision = jnp.zeros((), jnp.bfloat16)
    key_repeated = jnp.repeat(
        key_weight_matrix.reshape(local_row_count, KEY_VALUE_HEADS, HEAD_WIDTH),
        query_group_width,
        axis=1,
    ).reshape(local_row_count, tensor_parallel_count * HEAD_WIDTH)
    value_repeated = jnp.repeat(
        value_weight_matrix.reshape(local_row_count, KEY_VALUE_HEADS, HEAD_WIDTH),
        query_group_width,
        axis=1,
    ).reshape(local_row_count, tensor_parallel_count * HEAD_WIDTH)
    query_cols, key_cols, value_cols = (
        lax.all_to_all(w_query, "tp", split_axis=1, concat_axis=0, tiled=True),
        lax.all_to_all(key_repeated, "tp", split_axis=1, concat_axis=0, tiled=True),
        lax.all_to_all(value_repeated, "tp", split_axis=1, concat_axis=0, tiled=True),
    )
    key_bias = lax.dynamic_slice_in_dim(key_offset_bias, kv_head * HEAD_WIDTH, HEAD_WIDTH)
    value_bias = lax.dynamic_slice_in_dim(value_offset_bias, kv_head * HEAD_WIDTH, HEAD_WIDTH)
    key_projected_rows = jnp.dot(
        normed, key_cols, preferred_element_type=jnp.float32
    ) + key_bias.astype(jnp.float32)
    value_rounded_rows = (
        jnp.dot(normed, value_cols, preferred_element_type=jnp.float32)
        + value_bias.astype(jnp.float32)
    ).astype(jnp.bfloat16)
    value_cache = lax.dynamic_slice_in_dim(
        jnp.where(valid_token_mask[:, None], value_rounded_rows, zero_half_precision),
        offset,
        tile_width,
        1,
    )
    queries = jnp.dot(normed, query_cols, preferred_element_type=jnp.float32) + b_query.astype(
        jnp.float32
    )
    pos_float = jnp.tile(positions, GROUP_ROLLOUTS).astype(jnp.float32)
    inverse_freq = jnp.power(
        ROPE_BASE, -2.0 * jnp.arange(HEAD_WIDTH // 2).astype(jnp.float32) / HEAD_WIDTH
    )
    angles = pos_float[:, None] * inverse_freq[None, :]
    cosine_table = jnp.concatenate([jnp.cos(angles), jnp.cos(angles)], axis=-1)
    sine_table = jnp.concatenate([jnp.sin(angles), jnp.sin(angles)], axis=-1)
    query_rotated = rotary_tables(
        queries.reshape(token_count, heads_dev, HEAD_WIDTH), cosine_table, sine_table
    ).astype(jnp.bfloat16)
    key_rotated = (
        rotary_tables(
            key_projected_rows.reshape(token_count, 1, HEAD_WIDTH), cosine_table, sine_table
        )
        .reshape(token_count, HEAD_WIDTH)
        .astype(jnp.bfloat16)
    )
    rotated_key_cache = lax.dynamic_slice_in_dim(
        jnp.where(valid_token_mask[:, None], key_rotated, zero_half_precision),
        offset,
        tile_width,
        1,
    )
    q_heads = query_rotated.reshape(GROUP_ROLLOUTS, ROLLOUT_SLOTS, heads_dev, HEAD_WIDTH)
    k_heads = key_rotated.reshape(GROUP_ROLLOUTS, ROLLOUT_SLOTS, HEAD_WIDTH)
    v_heads = value_rounded_rows.reshape(GROUP_ROLLOUTS, ROLLOUT_SLOTS, HEAD_WIDTH)
    scores = jnp.einsum(
        "rthd,rsd->rhts", q_heads, k_heads, preferred_element_type=jnp.float32
    ) / jnp.sqrt(jnp.float32(HEAD_WIDTH))
    causal = positions[None, :] <= positions[:, None]
    scores = jnp.where(causal, scores, -jnp.inf)
    row_max = jnp.max(scores, axis=-1, keepdims=True)
    weights = jnp.exp(scores - row_max)
    attn_probs = (weights / jnp.sum(weights, axis=-1, keepdims=True)).astype(jnp.bfloat16)
    context = jnp.einsum("rhts,rsd->rthd", attn_probs, v_heads, preferred_element_type=jnp.float32)
    context = jnp.where(valid_grid[:, :, None, None], context, 0.0).astype(jnp.bfloat16)
    context = context.reshape(token_count, heads_dev * HEAD_WIDTH)
    summed = lax.psum_scatter(
        lax.dot_general(
            w_out, context, (((0,), (1,)), ((), ())), preferred_element_type=jnp.float32
        ),
        "tp",
        scatter_dimension=0,
        tiled=True,
    )
    attended = summed.T
    layer_out = (hidden_in.astype(jnp.float32) + attended).astype(jnp.bfloat16)
    return (layer_out, rotated_key_cache, value_cache)


def solution(mesh):
    in_specs = (
        P("grp", "tp"),
        P("tp"),
        P("tp", None),
        P("tp"),
        P("tp", None),
        P(),
        P("tp", None),
        P(),
        P("tp", None),
        P("grp"),
    )
    out_specs = (P("grp", "tp"), P("grp", "tp"), P("grp", "tp"))
    body = local_fused if mesh.shape["tp"] == 16 else local
    return jax.shard_map(body, mesh=mesh, in_specs=in_specs, out_specs=out_specs, check_vma=False)
```

```python
import jax
import jax.numpy as jnp
import numpy as np
from jax import lax
from jax.experimental import pallas as pl
from jax.experimental.pallas import tpu as pltpu
from jax.sharding import PartitionSpec as P

QUERY_HEADS = 64
KEY_VALUE_HEADS = 8
HEAD_WIDTH = 128
ROLLOUT_SLOTS = 192
GROUP_ROLLOUTS = 2


NORM_EPS = 1e-06
ROPE_BASE = 1000000.0
MODEL_WIDTH = 8192


BF = jnp.bfloat16
F32 = jnp.float32
MESH = pl.DeviceIdType.MESH
TOKENS = GROUP_ROLLOUTS * ROLLOUT_SLOTS
PARTNERS = (1, 2, 3, 4, 8, 12)
I16 = jnp.int16
CODED = TOKENS + 16


def flip(bit, mask):
    return bit + mask - 2 * bit * mask


def dotf(a, b):
    return jnp.dot(a, b, preferred_element_type=F32)


def code(ref, x):
    top = jnp.maximum(jnp.max(jnp.abs(x), axis=0, keepdims=True), 1e-30)
    exponent = jnp.ceil(jnp.log2(top))
    ref[0:TOKENS, :] = jnp.round(x * (32000.0 * jnp.exp2(-exponent))).astype(jnp.int32).astype(I16)
    ref[TOKENS:CODED, :] = jnp.broadcast_to(exponent, (16, x.shape[1])).astype(jnp.int32).astype(I16)


def decode(ref, rows=slice(0, TOKENS), cols=slice(None)):
    exponent = ref[TOKENS:CODED, cols].astype(jnp.int32).astype(F32)[0:1, :]
    return ref[rows, cols].astype(jnp.int32).astype(F32) * (jnp.exp2(exponent) * (1.0 / 32000.0))


def rotate(x, cos, sin_signed):
    return x * cos + pltpu.roll(x, HEAD_WIDTH // 2, 1) * sin_signed


def fused(
    len_ref, x_ref, gain_ref, bq_ref, kb_ref, vb_ref, cos_ref, sin_ref, wq, wk, wv, wo,
    out_ref, kc_ref, vc_ref,
    xb, gb, nx, wqb, wkvb, wob,
    r1, r1r, r2, r2r,
    yas, yar, ybs, ybr, own, zas, zar, zbs, zbr,
    kvbuf, ctxb, yos, yor, owno, zos, zor,
    l_q, l_o, l_kv, c_send, c_recv,
    wq_s, wq_r, wo_s, wo_r, r_s, r_r,
    y_s, y_r, z_s, z_r,
):
    me = lax.axis_index("tp")
    c = lax.rem(me, 2)
    y = lax.rem(me // 2, 2)
    zl = lax.rem(me // 4, 2)
    zh = me // 8

    def place(mask):
        return 8 * flip(zh, mask // 8) + 4 * flip(zl, mask // 4 % 2) + 2 * flip(y, mask // 2 % 2) + flip(c, mask % 2)

    def to(src, dst, ssem, rsem, mask):
        return pltpu.make_async_remote_copy(
            src_ref=src, dst_ref=dst, send_sem=ssem, recv_sem=rsem,
            device_id={"tp": place(mask)}, device_id_type=MESH,
        )

    def z_mask(i):
        return 3 - i

    def column(i, my, mc):
        return pl.ds(pl.multiple_of(place(4 * z_mask(i) + 2 * my + mc) * 512, 512), 512)

    def load(w, buf, sem, i, h):
        return pltpu.make_async_copy(w.at[:, column(i, 1 - h, 0)], buf.at[c, 2 * i + h], sem.at[2 * i + h])

    def swap(w, buf, ss, rs, i, h):
        return to(w.at[:, column(i, 1 - h, 1)], buf.at[c, 2 * i + h], ss.at[2 * i + h], rs.at[2 * i + h], 1)

    barrier = pltpu.get_barrier_semaphore()
    for mask in PARTNERS:
        pl.semaphore_signal(barrier, inc=1, device_id={"tp": place(mask)}, device_id_type=MESH)

    @pl.when(c == 0)
    def _():
        pltpu.make_async_copy(wk, wkvb.at[c], l_kv).start()

    @pl.when(c == 1)
    def _():
        pltpu.make_async_copy(wv, wkvb.at[c], l_kv).start()

    @pl.loop(0, 4)
    def _(i):
        load(wq, wqb, l_q, i, 0).start()
        load(wq, wqb, l_q, i, 1).start()

    xf = x_ref[...].astype(F32)
    sq = xf * xf
    sq = (sq[:, 0:128] + sq[:, 128:256]) + (sq[:, 256:384] + sq[:, 384:512])
    r1[...] = jnp.broadcast_to(jnp.sum(sq.T, axis=0, keepdims=True), (8, TOKENS))
    xb[pl.ds(c, 1)] = x_ref[...][None]
    gb[pl.ds(c, 1)] = jnp.broadcast_to(gain_ref[...].astype(F32).reshape(1, 512), (16, 512)).astype(BF)[None]

    pl.semaphore_wait(barrier, len(PARTNERS))

    for k in range(3):
        to(r1, r1r.at[k], r_s.at[k], r_r.at[k], k + 1).start()
    x_copy = to(x_ref, xb.at[c], c_send.at[0], c_recv.at[0], 1)
    g_copy = to(gb.at[c], gb.at[c], c_send.at[1], c_recv.at[1], 1)
    x_copy.start()
    g_copy.start()
    swap(wq, wqb, wq_s, wq_r, 0, 0).start()
    swap(wq, wqb, wq_s, wq_r, 0, 1).start()

    @pl.when(c == 0)
    def _():
        to(wv, wkvb.at[c], c_send.at[2], c_recv.at[2], 1).start()

    @pl.when(c == 1)
    def _():
        to(wk, wkvb.at[c], c_send.at[2], c_recv.at[2], 1).start()

    @pl.loop(1, 4)
    def _(i):
        swap(wq, wqb, wq_s, wq_r, i, 0).start()
        swap(wq, wqb, wq_s, wq_r, i, 1).start()

    for k in range(3):
        to(r1, r1r.at[k], r_s.at[k], r_r.at[k], k + 1).wait()
    r2[...] = (r1[...] + r1r[0]) + (r1r[1] + r1r[2])
    for k in range(3):
        to(r2, r2r.at[k], r_s.at[3 + k], r_r.at[3 + k], 4 * (k + 1)).start()
    for k in range(3):
        to(r2, r2r.at[k], r_s.at[3 + k], r_r.at[3 + k], 4 * (k + 1)).wait()
    total = (r2[...] + r2r[0]) + (r2r[1] + r2r[2])
    scale = lax.rsqrt(total[0:1, :] * (1.0 / MODEL_WIDTH) + NORM_EPS)
    scale = jnp.broadcast_to(scale, (128, TOKENS)).T
    x_copy.wait()
    g_copy.wait()
    for s in range(2):
        for b in range(4):
            cols = slice(128 * b, 128 * (b + 1))
            nx[s, :, cols] = (
                xb[s, :, cols].astype(F32) * scale * gb[s, 0:1, cols].astype(F32)
            ).astype(BF)

    @pl.loop(0, 4)
    def _(i):
        load(wo, wob, l_o, i, 0).start()
        load(wo, wob, l_o, i, 1).start()
        swap(wo, wob, wo_s, wo_r, i, 0).start()
        swap(wo, wob, wo_s, wo_r, i, 1).start()

    pltpu.make_async_copy(wk, wkvb.at[c], l_kv).wait()
    to(wk, wkvb.at[c], c_send.at[2], c_recv.at[2], 1).wait()

    def head(i, my):
        return pl.ds(pl.multiple_of(place(4 * z_mask(i) + 2 * my) // 2 * 128, 128), 128)

    def ya(i):
        return to(yas.at[i], yar.at[i], y_s.at[i], y_r.at[i], 2)

    def yb(i):
        return to(ybs.at[i], ybr.at[i], y_s.at[4 + i], y_r.at[4 + i], 2)

    def za(i):
        return to(zas.at[i], zar.at[i], z_s.at[i], z_r.at[i], 4 * z_mask(i))

    def zb(i):
        return to(zbs.at[i], zbr.at[i], z_s.at[3 + i], z_r.at[3 + i], 4 * z_mask(i))

    def yo(u):
        return to(yos.at[u], yor.at[u], y_s.at[8 + u], y_r.at[8 + u], 2)

    def zo(u):
        return to(zos.at[u], zor.at[u], z_s.at[6 + u], z_r.at[6 + u], 4 * z_mask(u // 2))

    left, right = slice(0, 256), slice(256, 512)

    def project(act, w, j, cols):
        return dotf(act[0], w[0, j, :, cols]) + dotf(act[1], w[1, j, :, cols])

    def project_kv(i, my):
        cols = head(i, my)
        return dotf(nx[0], wkvb[0, :, cols]) + dotf(nx[1], wkvb[1, :, cols])

    @pl.loop(0, 4)
    def _(i):
        load(wq, wqb, l_q, i, 0).wait()
        swap(wq, wqb, wq_s, wq_r, i, 0).wait()
        code(yas.at[i], project(nx, wqb, 2 * i, left))
        ya(i).start()
        code(ybs.at[i, :, 0:256], project(nx, wqb, 2 * i, right))
        code(ybs.at[i, :, 256:384], project_kv(i, 1))
        yb(i).start()

    def own_part(i):
        load(wq, wqb, l_q, i, 1).wait()
        swap(wq, wqb, wq_s, wq_r, i, 1).wait()
        own[:, left] = project(nx, wqb, 2 * i + 1, left)
        own[:, right] = project(nx, wqb, 2 * i + 1, right)
        own[:, 512:640] = project_kv(i, 0)

    @pl.loop(0, 3)
    def _(i):
        own_part(i)
        ya(i).wait()
        code(zas.at[i], own[:, left] + decode(yar.at[i]))
        za(i).start()
        yb(i).wait()
        code(zbs.at[i], own[:, 256:640] + decode(ybr.at[i]))
        zb(i).start()

    own_part(3)
    ya(3).wait()
    own[:, left] = own[:, left] + decode(yar.at[3])
    yb(3).wait()
    own[:, 256:640] = own[:, 256:640] + decode(ybr.at[3])
    for i in range(3):
        za(i).wait()
        zb(i).wait()
    kv = own[:, 512:640]
    for i in range(3):
        kv = kv + decode(zbr.at[i], cols=slice(256, 384))
    kv_row = lax.broadcasted_iota(jnp.int32, (KEY_VALUE_HEADS, HEAD_WIDTH), 0)
    core = jnp.full((TOKENS, HEAD_WIDTH), c, jnp.int32)
    bias = jnp.where(
        core[0:KEY_VALUE_HEADS] == 0,
        kb_ref[...].astype(F32).reshape(KEY_VALUE_HEADS, HEAD_WIDTH),
        vb_ref[...].astype(F32).reshape(KEY_VALUE_HEADS, HEAD_WIDTH),
    )
    kv = kv + jnp.sum(jnp.where(kv_row == me // 2, bias, 0.0), axis=0, keepdims=True)
    cos, sin_signed = cos_ref[...], sin_ref[...]
    kvbuf[pl.ds(c, 1)] = jnp.where(core == 0, rotate(kv, cos, sin_signed), kv).astype(BF)[None]
    kv_copy = to(kvbuf.at[c], kvbuf.at[c], c_send.at[3], c_recv.at[3], 1)
    kv_copy.start()

    row = lax.broadcasted_iota(jnp.int32, (TOKENS, HEAD_WIDTH), 0)
    ok = row < jnp.where(row < ROLLOUT_SLOTS, len_ref[0], len_ref[1] + ROLLOUT_SLOTS)
    half = HEAD_WIDTH // 2

    def cache(x):
        x = jnp.where(ok, x.astype(F32), 0.0)
        return jnp.where(core[:, :half] == 0, x[:, :half], x[:, half:]).T.astype(BF)

    kv_copy.wait()
    kc_ref[...] = cache(kvbuf[0])
    vc_ref[...] = cache(kvbuf[1])

    shape = (ROLLOUT_SLOTS, ROLLOUT_SLOTS)
    causal = lax.broadcasted_iota(jnp.int32, shape, 1) <= lax.broadcasted_iota(jnp.int32, shape, 0)
    bq = bq_ref[...].astype(F32).reshape(1, 512)
    for r in range(GROUP_ROLLOUTS):
        rows = slice(ROLLOUT_SLOTS * r, ROLLOUT_SLOTS * (r + 1))
        k, v = kvbuf[0, rows, :], kvbuf[1, rows, :]
        for h in range(4):
            cols = slice(128 * h, 128 * (h + 1))
            zr, zcols = (zar, cols) if h < 2 else (zbr, slice(cols.start - 256, cols.stop - 256))
            q = own[rows, cols] + decode(zr.at[0], rows, zcols)
            q = q + (decode(zr.at[1], rows, zcols) + decode(zr.at[2], rows, zcols))
            q = q + bq[:, cols]
            q = rotate(q, cos[rows], sin_signed[rows]).astype(BF)
            s = lax.dot_general(q, k, (((1,), (1,)), ((), ())), preferred_element_type=F32)
            s = jnp.where(causal, s / np.float32(np.sqrt(np.float32(HEAD_WIDTH))), -jnp.inf)
            w = jnp.exp(s - jnp.max(s, axis=1, keepdims=True))
            p = (w / jnp.sum(w, axis=1, keepdims=True)).astype(BF)
            o = jnp.where(ok[rows], dotf(p, v), 0.0).astype(BF)
            ctxb[pl.ds(c, 1), rows, cols] = o[None]
    ctx_copy = to(ctxb.at[c], ctxb.at[c], c_send.at[4], c_recv.at[4], 1)
    ctx_copy.start()
    ctx_copy.wait()

    @pl.loop(0, 4)
    def _(i):
        load(wo, wob, l_o, i, 0).wait()
        swap(wo, wob, wo_s, wo_r, i, 0).wait()
        code(yos.at[2 * i], project(ctxb, wob, 2 * i, left))
        yo(2 * i).start()
        code(yos.at[2 * i + 1], project(ctxb, wob, 2 * i, right))
        yo(2 * i + 1).start()

    def own_out(i):
        load(wo, wob, l_o, i, 1).wait()
        swap(wo, wob, wo_s, wo_r, i, 1).wait()
        owno[:, left] = project(ctxb, wob, 2 * i + 1, left)
        owno[:, right] = project(ctxb, wob, 2 * i + 1, right)

    @pl.loop(0, 3)
    def _(i):
        own_out(i)
        yo(2 * i).wait()
        code(zos.at[2 * i], owno[:, left] + decode(yor.at[2 * i]))
        zo(2 * i).start()
        yo(2 * i + 1).wait()
        code(zos.at[2 * i + 1], owno[:, right] + decode(yor.at[2 * i + 1]))
        zo(2 * i + 1).start()

    own_out(3)
    for p, cols in enumerate((left, right)):
        yo(6 + p).wait()
        att = owno[:, cols] + decode(yor.at[6 + p])
        for i in range(3):
            zo(2 * i + p).wait()
            att = att + decode(zor.at[2 * i + p])
        out_ref[:, cols] = (x_ref[:, cols].astype(F32) + att).astype(BF)


def local_fused(
    hidden_in, norm_gain, w_query, b_query, key_weight_matrix, key_offset_bias,
    value_weight_matrix, value_offset_bias, w_out, lengths,
):
    positions = np.tile(np.arange(ROLLOUT_SLOTS), GROUP_ROLLOUTS).astype(np.float64)
    freq = ROPE_BASE ** (-2.0 * np.arange(HEAD_WIDTH // 2) / HEAD_WIDTH)
    angles = positions[:, None] * freq[None, :]
    cos = np.concatenate([np.cos(angles), np.cos(angles)], axis=1).astype(np.float32)
    sin_signed = np.concatenate([-np.sin(angles), np.sin(angles)], axis=1).astype(np.float32)
    vmem = pl.BlockSpec(memory_space=pltpu.VMEM)
    hbm = pl.BlockSpec(memory_space=pl.ANY)
    sem = pltpu.SemaphoreType.DMA
    V = pltpu.VMEM
    T = TOKENS
    out, kc, vc = pl.pallas_call(
        fused,
        out_shape=(
            jax.ShapeDtypeStruct((T, 512), BF),
            jax.ShapeDtypeStruct((HEAD_WIDTH // 2, T), BF),
            jax.ShapeDtypeStruct((HEAD_WIDTH // 2, T), BF),
        ),
        in_specs=[pl.BlockSpec(memory_space=pltpu.SMEM)] + [vmem] * 7 + [hbm] * 4,
        out_specs=(vmem, vmem, vmem),
        scratch_shapes=[
            V((2, T, 512), BF), V((2, 16, 512), BF), V((2, T, 512), BF),
            V((2, 8, 512, 512), BF), V((2, 512, 1024), BF), V((2, 8, 512, 512), BF),
            V((8, T), F32), V((3, 8, T), F32), V((8, T), F32), V((3, 8, T), F32),
            V((4, CODED, 256), I16), V((4, CODED, 256), I16), V((4, CODED, 384), I16), V((4, CODED, 384), I16),
            V((T, 640), F32),
            V((3, CODED, 256), I16), V((3, CODED, 256), I16), V((3, CODED, 384), I16), V((3, CODED, 384), I16),
            V((2, T, 128), BF), V((2, T, 512), BF),
            V((8, CODED, 256), I16), V((8, CODED, 256), I16), V((T, 512), F32),
            V((6, CODED, 256), I16), V((6, CODED, 256), I16),
            sem((8,)), sem((8,)), sem, sem((5,)), sem((5,)),
            sem((8,)), sem((8,)), sem((8,)), sem((8,)), sem((6,)), sem((6,)),
            sem((16,)), sem((16,)), sem((12,)), sem((12,)),
        ],
        compiler_params=pltpu.CompilerParams(
            collective_id=0, has_side_effects=True, vmem_limit_bytes=56 * 1024 * 1024
        ),
    )(
        lengths, hidden_in, norm_gain, b_query, key_offset_bias, value_offset_bias,
        jnp.asarray(cos), jnp.asarray(sin_signed),
        w_query, key_weight_matrix, value_weight_matrix, w_out,
    )
    return out, kc.T, vc.T


def rotary_tables(values, cosine_table, sine_table):
    half_dim = values.shape[-1] // 2
    first_half = values[..., :half_dim]
    second_half = values[..., half_dim:]
    turned = jnp.concatenate([-second_half, first_half], axis=-1)
    return values * cosine_table[:, None, :] + turned * sine_table[:, None, :]


def local(
    hidden_in,
    norm_gain,
    w_query,
    b_query,
    key_weight_matrix,
    key_offset_bias,
    value_weight_matrix,
    value_offset_bias,
    w_out,
    lengths,
):
    tensor_parallel_count = lax.axis_size("tp")
    device_place = lax.axis_index("tp")
    query_group_width = tensor_parallel_count // KEY_VALUE_HEADS
    heads_dev = QUERY_HEADS // tensor_parallel_count
    token_count = hidden_in.shape[0]
    gathered, gain_all = (
        lax.all_gather(hidden_in, "tp", axis=1, tiled=True),
        lax.all_gather(norm_gain, "tp", axis=0, tiled=True),
    )
    full_x = gathered.astype(jnp.float32)
    mean_square = jnp.mean(full_x * full_x, axis=-1, keepdims=True)
    normed = (full_x * lax.rsqrt(mean_square + NORM_EPS) * gain_all.astype(jnp.float32)).astype(
        jnp.bfloat16
    )
    local_row_count = key_weight_matrix.shape[0]
    kv_head = device_place // query_group_width
    tile_width = HEAD_WIDTH // query_group_width
    offset = device_place % query_group_width * tile_width
    positions = jnp.arange(ROLLOUT_SLOTS, dtype=jnp.int32)
    valid_grid = positions[None, :] < lengths[:, None]
    valid_token_mask = valid_grid.reshape(-1)
    zero_half_precision = jnp.zeros((), jnp.bfloat16)
    key_repeated = jnp.repeat(
        key_weight_matrix.reshape(local_row_count, KEY_VALUE_HEADS, HEAD_WIDTH),
        query_group_width,
        axis=1,
    ).reshape(local_row_count, tensor_parallel_count * HEAD_WIDTH)
    value_repeated = jnp.repeat(
        value_weight_matrix.reshape(local_row_count, KEY_VALUE_HEADS, HEAD_WIDTH),
        query_group_width,
        axis=1,
    ).reshape(local_row_count, tensor_parallel_count * HEAD_WIDTH)
    query_cols, key_cols, value_cols = (
        lax.all_to_all(w_query, "tp", split_axis=1, concat_axis=0, tiled=True),
        lax.all_to_all(key_repeated, "tp", split_axis=1, concat_axis=0, tiled=True),
        lax.all_to_all(value_repeated, "tp", split_axis=1, concat_axis=0, tiled=True),
    )
    key_bias = lax.dynamic_slice_in_dim(key_offset_bias, kv_head * HEAD_WIDTH, HEAD_WIDTH)
    value_bias = lax.dynamic_slice_in_dim(value_offset_bias, kv_head * HEAD_WIDTH, HEAD_WIDTH)
    key_projected_rows = jnp.dot(
        normed, key_cols, preferred_element_type=jnp.float32
    ) + key_bias.astype(jnp.float32)
    value_rounded_rows = (
        jnp.dot(normed, value_cols, preferred_element_type=jnp.float32)
        + value_bias.astype(jnp.float32)
    ).astype(jnp.bfloat16)
    value_cache = lax.dynamic_slice_in_dim(
        jnp.where(valid_token_mask[:, None], value_rounded_rows, zero_half_precision),
        offset,
        tile_width,
        1,
    )
    queries = jnp.dot(normed, query_cols, preferred_element_type=jnp.float32) + b_query.astype(
        jnp.float32
    )
    pos_float = jnp.tile(positions, GROUP_ROLLOUTS).astype(jnp.float32)
    inverse_freq = jnp.power(
        ROPE_BASE, -2.0 * jnp.arange(HEAD_WIDTH // 2).astype(jnp.float32) / HEAD_WIDTH
    )
    angles = pos_float[:, None] * inverse_freq[None, :]
    cosine_table = jnp.concatenate([jnp.cos(angles), jnp.cos(angles)], axis=-1)
    sine_table = jnp.concatenate([jnp.sin(angles), jnp.sin(angles)], axis=-1)
    query_rotated = rotary_tables(
        queries.reshape(token_count, heads_dev, HEAD_WIDTH), cosine_table, sine_table
    ).astype(jnp.bfloat16)
    key_rotated = (
        rotary_tables(
            key_projected_rows.reshape(token_count, 1, HEAD_WIDTH), cosine_table, sine_table
        )
        .reshape(token_count, HEAD_WIDTH)
        .astype(jnp.bfloat16)
    )
    rotated_key_cache = lax.dynamic_slice_in_dim(
        jnp.where(valid_token_mask[:, None], key_rotated, zero_half_precision),
        offset,
        tile_width,
        1,
    )
    q_heads = query_rotated.reshape(GROUP_ROLLOUTS, ROLLOUT_SLOTS, heads_dev, HEAD_WIDTH)
    k_heads = key_rotated.reshape(GROUP_ROLLOUTS, ROLLOUT_SLOTS, HEAD_WIDTH)
    v_heads = value_rounded_rows.reshape(GROUP_ROLLOUTS, ROLLOUT_SLOTS, HEAD_WIDTH)
    scores = jnp.einsum(
        "rthd,rsd->rhts", q_heads, k_heads, preferred_element_type=jnp.float32
    ) / jnp.sqrt(jnp.float32(HEAD_WIDTH))
    causal = positions[None, :] <= positions[:, None]
    scores = jnp.where(causal, scores, -jnp.inf)
    row_max = jnp.max(scores, axis=-1, keepdims=True)
    weights = jnp.exp(scores - row_max)
    attn_probs = (weights / jnp.sum(weights, axis=-1, keepdims=True)).astype(jnp.bfloat16)
    context = jnp.einsum("rhts,rsd->rthd", attn_probs, v_heads, preferred_element_type=jnp.float32)
    context = jnp.where(valid_grid[:, :, None, None], context, 0.0).astype(jnp.bfloat16)
    context = context.reshape(token_count, heads_dev * HEAD_WIDTH)
    summed = lax.psum_scatter(
        lax.dot_general(
            w_out, context, (((0,), (1,)), ((), ())), preferred_element_type=jnp.float32
        ),
        "tp",
        scatter_dimension=0,
        tiled=True,
    )
    attended = summed.T
    layer_out = (hidden_in.astype(jnp.float32) + attended).astype(jnp.bfloat16)
    return (layer_out, rotated_key_cache, value_cache)


def solution(mesh):
    in_specs = (
        P("grp", "tp"),
        P("tp"),
        P("tp", None),
        P("tp"),
        P("tp", None),
        P(),
        P("tp", None),
        P(),
        P("tp", None),
        P("grp"),
    )
    out_specs = (P("grp", "tp"), P("grp", "tp"), P("grp", "tp"))
    body = local_fused if mesh.shape["tp"] == 16 else local
    return jax.shard_map(body, mesh=mesh, in_specs=in_specs, out_specs=out_specs, check_vma=False)
```
